32 devices in a mesh: parts: 2 (over y), expert: 4 (over z), dp: 4 (over x, core).
Axes of the slice: x: 2, y: 2, z: 4, core: 2. Of those that a mesh axis runs over, the one named last changes fastest.
Arguments:
- tokens: bfloat16 [256, 6144], P(('parts', 'expert'), 'dp'), parts along dimension 0, may hold values from -6 to 6
- cotangent: bfloat16 [256, 6144], P(('parts', 'expert'), 'dp'), parts along dimension 0, may hold values from -6 to 6
- w_gate: bfloat16 [4, 6144, 8192], P('parts', 'dp', 'expert'), parts along dimension 0, may hold values from -0.078125 to 0.078125
- w_up: bfloat16 [4, 6144, 8192], P('parts', 'dp', 'expert'), parts along dimension 0, may hold values from -0.078125 to 0.078125
- w_down: bfloat16 [4, 8192, 6144], P('parts', 'expert', 'dp'), parts along dimension 0, may hold values from -0.0625 to 0.0625
- gate_table: float32 [64, 2], replicated, may hold values from 0.1 to 1
- expert_ids: int32 [256, 2], P('parts'), parts along dimension 0, may hold values from 0 to 7, as said below
- gate_index: int32 [256], P('parts'), parts along dimension 0, may hold values from 0 to 63
- hot_ids: int32 [4], P('parts'), parts along dimension 0, may hold values from 0 to 7, as said below
Outputs:
- mixed: bfloat16 [256, 6144], P(('parts', 'expert'), 'dp'), parts along dimension 0
- grad_tokens: bfloat16 [256, 6144], P(('parts', 'expert'), 'dp'), parts along dimension 0
- grad_gate: bfloat16 [4, 6144, 8192], P('parts', 'dp', 'expert'), parts along dimension 0
- grad_up: bfloat16 [4, 6144, 8192], P('parts', 'dp', 'expert'), parts along dimension 0
- grad_down: bfloat16 [4, 8192, 6144], P('parts', 'expert', 'dp'), parts along dimension 0
The draws below stay inside these ranges and needn't reach their ends.
There are 2 independent parts, one for each index of `parts`. The reference program is written for one: setup_inputs(seed, part) draws one part's arguments, and reference() takes and returns one part's arrays. A program takes and returns all parts, laid end to end along the dimension named above; an argument that names none is the same for every part. Nothing has to cross between parts.
Inputs may be any that keep to these rules, and one draw needn't show every extreme that they name: `expert_ids`: each row names two different experts. `hot_ids`: two different experts.
All inputs are finite; a program needn't handle non-finite values.
Results may differ from the reference program's by a relative error of at most 0.0095.
Values may be sent and summed in bfloat16 or wider, within the bound.
A program may use at most 192 MiB of HBM per device.

```python
import jax
import jax.numpy as jnp
from jax import lax

D = 6144
FF = 8192
EXPERTS = 8
TOP = 2
HOT = 2
NTAB = 64
TOKENS = 128
N_EXPERT = 4


def hot_pair(key):
    first = jax.random.randint(jax.random.fold_in(key, 11), (), 0, EXPERTS)
    offset = jax.random.randint(jax.random.fold_in(key, 12), (), 1, EXPERTS)
    second = (first + offset) % EXPERTS
    return jnp.stack([first, second]).astype(jnp.int32)


def draw_hot_ids(key, part):
    return hot_pair(key)


def draw_expert_ids(key, part):
    chosen = hot_pair(key)
    key = jax.random.fold_in(key, 5)
    choose_kind = jax.random.randint(jax.random.fold_in(key, 1), (TOKENS,), 0, 8)
    which_hot = jax.random.randint(jax.random.fold_in(key, 2), (TOKENS,), 0, 2)
    any_first = jax.random.randint(jax.random.fold_in(key, 3), (TOKENS,), 0, EXPERTS)
    first = jnp.where(choose_kind < 6, chosen[which_hot], any_first)
    second_kind = jax.random.randint(jax.random.fold_in(key, 4), (TOKENS,), 0, 2)
    offset = jax.random.randint(jax.random.fold_in(key, 6), (TOKENS,), 1, EXPERTS)
    other_hot = chosen[1 - which_hot]
    random_second = (first + offset) % EXPERTS
    second = jnp.where((second_kind == 0) & (other_hot != first), other_hot, random_second)
    return jnp.stack([first, second], axis=1).astype(jnp.int32)


def set_ends(array, key, least, largest):
    longest = array.shape.index(max(array.shape))
    spots = []
    for shift in (0, 1):
        where = [jax.random.randint(jax.random.fold_in(key, axis), (), 0, length) for axis, length in enumerate(array.shape)]
        where[longest] = (where[longest] + shift) % array.shape[longest]
        spots.append(tuple(where))
    return array.at[spots[0]].set(least).at[spots[1]].set(largest)


def level_of(own_key, dims, shards, smallest, high):
    gain, own = 1.0, jax.random.fold_in(own_key, 6)
    for position, blocks in shards:
        draws = jnp.exp(jax.random.uniform(jax.random.fold_in(own, position), (blocks,), jnp.float32, smallest / len(shards), high / len(shards)))
        gain = gain * jnp.repeat(draws, dims[position] // blocks).reshape([-1 if axis == position else 1 for axis in range(len(dims))])
    return gain


def normal_values(rng, dims, scale, most, cuts=(), held_as=jnp.bfloat16):
    drawn = scale * jax.random.normal(rng, dims, jnp.float32)
    if cuts:
        drawn = drawn * level_of(rng, dims, cuts, -0.22, 0.18)
    return jnp.clip(drawn, -most, most).astype(held_as)


def setup_inputs(seed: int = 0, part: int = 0) -> dict:
    key_of = jax.random.split(jax.random.key(seed), 10)
    part_keys = jax.random.split(jax.random.fold_in(key_of[9], part), 10)
    return {
        "tokens": normal_values(part_keys[0], (TOKENS, D), 1.0, 6.0, ((0, 4), (1, 4))),
        "cotangent": normal_values(part_keys[1], (TOKENS, D), 1.0, 6.0, ((0, 4), (1, 4))),
        "w_gate": normal_values(part_keys[2], (HOT, D, FF), D ** -0.5, 0.078125, ((1, 4), (2, 4))),
        "w_up": normal_values(part_keys[3], (HOT, D, FF), D ** -0.5, 0.078125, ((1, 4), (2, 4))),
        "w_down": normal_values(part_keys[4], (HOT, FF, D), FF ** -0.5, 0.0625, ((1, 4), (2, 4))),
        "gate_table": jnp.clip(jax.random.uniform(key_of[5], (NTAB, TOP), jnp.float32, 0.1, 1.0), 0.1, 1.0),
        "expert_ids": draw_expert_ids(jax.random.fold_in(jax.random.fold_in(key_of[9], part), 71), part),
        "gate_index": set_ends(jax.random.randint(part_keys[7], (TOKENS,), 0, NTAB), jax.random.fold_in(part_keys[7], 1), 0, NTAB - 1).astype(jnp.int32),
        "hot_ids": draw_hot_ids(jax.random.fold_in(jax.random.fold_in(key_of[9], part), 71), part),
    }


def routing_weight(gate_table, expert_ids, gate_index, hot_ids):
    gates = gate_table[gate_index]
    match = expert_ids[:, :, None] == hot_ids[None, None, :]
    return jnp.sum(jnp.where(match, gates[:, :, None], jnp.float32(0.0)), axis=1)


def block_total(lefts, rights):
    width = FF // N_EXPERT
    left_blocks = jnp.stack([item.reshape(TOKENS, N_EXPERT, width).transpose(1, 0, 2) for item in lefts], axis=1)
    right_blocks = jnp.stack([item.reshape(N_EXPERT, width, D) for item in rights], axis=1)

    def step(total, pair):
        left, right = pair
        term = jnp.zeros((TOKENS, D), jnp.float32)
        for index in range(len(lefts)):
            term = term + jnp.dot(left[index], right[index], preferred_element_type=jnp.float32)
        rounded = lax.optimization_barrier(term.astype(jnp.bfloat16))
        return total + rounded.astype(jnp.float32), None

    total, unused = lax.scan(step, jnp.zeros((TOKENS, D), jnp.float32), (left_blocks, right_blocks))
    return total.astype(jnp.bfloat16)


def reference(tokens, cotangent, w_gate, w_up, w_down, gate_table, expert_ids, gate_index, hot_ids):
    weight = routing_weight(gate_table, expert_ids, gate_index, hot_ids)
    products, d_gates, d_ups = [], [], []
    for index in range(HOT):
        pre_gate = jnp.dot(tokens, w_gate[index], preferred_element_type=jnp.float32)
        pre_up = jnp.dot(tokens, w_up[index], preferred_element_type=jnp.float32)
        sigma = jax.nn.sigmoid(pre_gate)
        scale = weight[:, index][:, None]
        products.append((scale * pre_gate * sigma * pre_up).astype(jnp.bfloat16))
        back = jnp.dot(cotangent, w_down[index].T, preferred_element_type=jnp.float32)
        d_gates.append((scale * back * pre_up * sigma * (1.0 + pre_gate * (1.0 - sigma))).astype(jnp.bfloat16))
        d_ups.append((scale * back * pre_gate * sigma).astype(jnp.bfloat16))
    mixed = block_total(products, [w_down[index] for index in range(HOT)])
    grad_tokens = block_total(d_gates + d_ups, [w_gate[index].T for index in range(HOT)] + [w_up[index].T for index in range(HOT)])
    grad_gate = jnp.stack([jnp.dot(tokens.T, d_gates[index], preferred_element_type=jnp.float32) for index in range(HOT)]).astype(jnp.bfloat16)
    grad_up = jnp.stack([jnp.dot(tokens.T, d_ups[index], preferred_element_type=jnp.float32) for index in range(HOT)]).astype(jnp.bfloat16)
    grad_down = jnp.stack([jnp.dot(products[index].T, cotangent, preferred_element_type=jnp.float32) for index in range(HOT)]).astype(jnp.bfloat16)
    return mixed, grad_tokens, grad_gate, grad_up, grad_down
```

```python
import functools

import jax
import jax.numpy as jnp
from jax import lax
from jax.experimental import pallas as pl
from jax.experimental.pallas import tpu as pltpu
from jax.sharding import PartitionSpec as P

MESH = pl.DeviceIdType.MESH
BF16, F32 = jnp.bfloat16, jnp.float32


def routing_weight(gate_table, expert_ids, gate_index, hot_ids):
    table_rows = gate_table.shape[0]
    select = gate_index[:, None] == jnp.arange(table_rows, dtype=jnp.int32)[None, :]
    gates = jnp.sum(jnp.where(select[:, :, None], gate_table[None, :, :], jnp.float32(0.0)), axis=1)
    match = expert_ids[:, :, None] == hot_ids[None, None, :]
    return jnp.sum(jnp.where(match, gates[:, :, None], jnp.float32(0.0)), axis=1)


def dot(a, b):
    return jnp.dot(a, b, preferred_element_type=F32)


def dot_nt(a, b):
    return lax.dot_general(a, b, (((1,), (1,)), ((), ())), preferred_element_type=F32)


def layer_kernel(
    n_expert, chunks, lead,
    tok_ref, cot_ref, wt_ref, wg_hbm, wu_hbm, wd_hbm,
    x_out, act_out, part_out,
    wg, wu, wd, xall, own, send1, recv1, send2, recv2, act, acc, part,
    w_sem, x_send, x_recv, s1, r1, s2, r2, s3, r3, out_sem, act_sem,
):
    rows, width = tok_ref.shape
    f = wg.shape[3]
    z = lax.axis_index("expert")
    dp = lax.axis_index("dp")
    mine = lax.rem(dp, 2)
    other = 1 - mine
    near = dp + 1 - 2 * mine
    far = lax.rem(dp + 2, 4)

    def load(k, h, s):
        cols = pl.ds(pl.multiple_of(s * f, f), f)
        if k == 2:
            src, dst = wd_hbm.at[h, cols, :], wd.at[h, s]
        else:
            src, dst = (wg_hbm, wu_hbm)[k].at[h, :, cols], (wg, wu)[k].at[h, s]
        return pltpu.make_async_copy(src, dst, w_sem.at[k, h, s])

    def load_gu(s, carry):
        for h in (other, mine):
            load(0, h, s).start()
            load(1, h, s).start()
        return carry

    def load_down(s, carry):
        for h in (other, mine):
            load(2, h, s).start()
        return carry

    def gather(k, step):
        peer = lax.rem(z + step, n_expert)
        mine_rows = pl.ds(pl.multiple_of(z * rows, rows), rows)
        return pltpu.make_async_remote_copy(
            src_ref=(tok_ref, cot_ref)[k],
            dst_ref=xall.at[k, mine_rows, :],
            send_sem=x_send.at[k, step],
            recv_sem=x_recv.at[k, step],
            device_id={"expert": peer},
            device_id_type=MESH,
        )

    barrier = pltpu.get_barrier_semaphore()

    def greet(step, carry):
        pl.semaphore_signal(
            barrier, inc=1, device_id={"expert": lax.rem(z + step, n_expert)}, device_id_type=MESH
        )
        return carry

    lax.fori_loop(0, lead, load_gu, 0)
    lax.fori_loop(1, n_expert, greet, 0)
    pl.semaphore_signal(barrier, inc=1, device_id={"dp": near}, device_id_type=MESH)
    pl.semaphore_signal(barrier, inc=1, device_id={"dp": far}, device_id_type=MESH)
    pl.semaphore_wait(barrier, n_expert + 1)

    for k in range(2):
        def send_rows(step, carry, k=k):
            gather(k, step).start()
            return carry
        lax.fori_loop(1, n_expert, send_rows, 0)

    def later(s, carry):
        load_down(s, 0)

        @pl.when(s + lead < chunks)
        def _():
            load_gu(s + lead, 0)
        return carry

    lax.fori_loop(0, chunks, later, 0)
    own_rows = pl.ds(pl.multiple_of(z * rows, rows), rows)
    xall[0, own_rows, :] = tok_ref[...]
    xall[1, own_rows, :] = cot_ref[...]
    acc[...] = jnp.zeros_like(acc)

    def arrive(k):
        def body(step, carry):
            gather(k, step).wait_recv()
            return carry
        lax.fori_loop(1, n_expert, body, 0)
        pltpu.make_async_copy(xall.at[k], x_out.at[k], out_sem.at[k]).start()

    span = (pl.ds(0, 2), pl.ds(2, 1))

    def to_near(g, s):
        return pltpu.make_async_remote_copy(
            src_ref=send1.at[s, span[g]], dst_ref=recv1.at[s, span[g]],
            send_sem=s1.at[g, s], recv_sem=r1.at[g, s],
            device_id={"dp": near}, device_id_type=MESH,
        )

    def to_far(g, s):
        return pltpu.make_async_remote_copy(
            src_ref=send2.at[s, span[g]], dst_ref=recv2.at[s, span[g]],
            send_sem=s2.at[g, s], recv_sem=r2.at[g, s],
            device_id={"dp": far}, device_id_type=MESH,
        )

    def act_to_near(h, s):
        return pltpu.make_async_remote_copy(
            src_ref=act.at[h, s], dst_ref=act.at[h, s],
            send_sem=s3.at[s], recv_sem=r3.at[s],
            device_id={"dp": near}, device_id_type=MESH,
        )

    def act_copy(h, s):
        cols = pl.ds(pl.multiple_of(s * f, f), f)
        return pltpu.make_async_copy(act.at[h, s], act_out.at[h, :, :, cols], act_sem.at[h, s])

    def gate_up(s):
        for k, w in ((0, wg), (1, wu)):
            load(k, other, s).wait()
            send1[s, k] = dot(xall[0], w[other, s]).astype(BF16)
        to_near(0, s).start()
        for k, w in ((0, wg), (1, wu)):
            load(k, mine, s).wait()
            own[s, k] = dot(xall[0], w[mine, s])

    def back(s):
        load(2, other, s).wait()
        send1[s, 2] = dot_nt(xall[1], wd[other, s]).astype(BF16)
        to_near(1, s).start()
        load(2, mine, s).wait()
        own[s, 2] = dot_nt(xall[1], wd[mine, s])

    def pair(g, s):
        to_near(g, s).wait_recv()
        for k in ((0, 1), (2,))[g]:
            both = own[s, k] + recv1[s, k].astype(F32)
            own[s, k] = both
            send2[s, k] = both.astype(BF16)
        to_far(g, s).start()

    arrive(0)

    def first(s, carry):
        @pl.when(s < chunks)
        def _():
            gate_up(s)

        @pl.when((s >= 1) & (s <= chunks))
        def _():
            pair(0, s - 1)

        @pl.when(s == lead)
        def _():
            arrive(1)

        @pl.when((s >= lead) & (s < chunks + lead))
        def _():
            back(s - lead)

        @pl.when(s >= lead + 1)
        def _():
            pair(1, s - lead - 1)
        return carry

    lax.fori_loop(0, chunks + lead + 1, first, 0)

    def project(h, s):
        acc[0] += dot(act[h, s, 0], wd[h, s])
        acc[1] += dot_nt(act[h, s, 1], wg[h, s]) + dot_nt(act[h, s, 2], wu[h, s])

    def second(s, carry):
        @pl.when(s < chunks)
        def _():
            to_far(0, s).wait_recv()
            to_far(1, s).wait_recv()
            weight = wt_ref[mine]
            gate = own[s, 0] + recv2[s, 0].astype(F32)
            up = own[s, 1] + recv2[s, 1].astype(F32)
            scaled = weight * (own[s, 2] + recv2[s, 2].astype(F32))
            sigma = jax.nn.sigmoid(gate)
            silu = gate * sigma
            act[mine, s, 0] = (weight * silu * up).astype(BF16)
            act[mine, s, 1] = (scaled * up * (sigma * (1.0 + gate * (1.0 - sigma)))).astype(BF16)
            act[mine, s, 2] = (scaled * silu).astype(BF16)
            act_to_near(mine, s).start()
            act_copy(mine, s).start()
            project(mine, s)

        @pl.when(s >= 1)
        def _():
            act_to_near(other, s - 1).wait_recv()
            act_copy(other, s - 1).start()
            project(other, s - 1)
        return carry

    lax.fori_loop(0, chunks + 1, second, 0)

    part[:, :width] = acc[0].astype(BF16)
    part[:, width:] = acc[1].astype(BF16)
    last = pltpu.make_async_copy(part, part_out, out_sem.at[2])
    last.start()

    def drain(s, carry):
        for g in range(2):
            to_near(g, s).wait_send()
            to_far(g, s).wait_send()
        act_to_near(mine, s).wait_send()
        for h in range(2):
            act_copy(h, s).wait()
        return carry

    lax.fori_loop(0, chunks, drain, 0)

    def drain_rows(step, carry):
        for k in range(2):
            gather(k, step).wait_send()
        return carry

    lax.fori_loop(1, n_expert, drain_rows, 0)
    for k in range(2):
        pltpu.make_async_copy(xall.at[k], x_out.at[k], out_sem.at[k]).wait()
    last.wait()


def grads_kernel(x_ref, act_ref, gg_ref, gu_ref, gd_ref, tok_t):
    @pl.when((pl.program_id(0) == 0) & (pl.program_id(1) == 0))
    def _():
        tok_t[...] = x_ref[0].T

    gg_ref[0] = dot(tok_t[...], act_ref[0, 1]).astype(BF16)
    gu_ref[0] = dot(tok_t[...], act_ref[0, 2]).astype(BF16)
    gd_ref[0] = dot(act_ref[0, 0].T, x_ref[1]).astype(BF16)


def local(n_expert, tokens, cotangent, w_gate, w_up, w_down, gate_table, expert_ids, gate_index, hot_ids):
    rows, width = tokens.shape
    hot, _, hidden = w_gate.shape
    total = rows * n_expert
    f = min(256, hidden)
    chunks = hidden // f
    lead = chunks // 2
    weight = routing_weight(gate_table, expert_ids, gate_index, hot_ids).T[:, :, None]
    vmem, anywhere = pl.BlockSpec(memory_space=pltpu.VMEM), pl.BlockSpec(memory_space=pl.ANY)
    dma = pltpu.SemaphoreType.DMA
    x_all, acts, partial = pl.pallas_call(
        functools.partial(layer_kernel, n_expert, chunks, lead),
        out_shape=(
            jax.ShapeDtypeStruct((2, total, width), BF16),
            jax.ShapeDtypeStruct((hot, 3, total, hidden), BF16),
            jax.ShapeDtypeStruct((total, 2 * width), BF16),
        ),
        in_specs=[vmem, vmem, vmem, anywhere, anywhere, anywhere],
        out_specs=(anywhere, anywhere, anywhere),
        scratch_shapes=[
            pltpu.VMEM((hot, chunks, width, f), BF16),
            pltpu.VMEM((hot, chunks, width, f), BF16),
            pltpu.VMEM((hot, chunks, f, width), BF16),
            pltpu.VMEM((2, total, width), BF16),
            pltpu.VMEM((chunks, 3, total, f), F32),
            pltpu.VMEM((chunks, 3, total, f), BF16),
            pltpu.VMEM((chunks, 3, total, f), BF16),
            pltpu.VMEM((chunks, 3, total, f), BF16),
            pltpu.VMEM((chunks, 3, total, f), BF16),
            pltpu.VMEM((hot, chunks, 3, total, f), BF16),
            pltpu.VMEM((2, total, width), F32),
            pltpu.VMEM((total, 2 * width), BF16),
            dma((3, hot, chunks)),
            dma((2, n_expert)),
            dma((2, n_expert)),
            dma((2, chunks)),
            dma((2, chunks)),
            dma((2, chunks)),
            dma((2, chunks)),
            dma((chunks,)),
            dma((chunks,)),
            dma((3,)),
            dma((hot, chunks)),
        ],
        compiler_params=pltpu.CompilerParams(
            collective_id=0, has_side_effects=True, vmem_limit_bytes=60 * 1024 * 1024
        ),
    )(tokens, cotangent, weight, w_gate, w_up, w_down)
    reduced = lax.psum_scatter(partial, "expert", scatter_dimension=0, tiled=True)
    grad_gate, grad_up, grad_down = pl.pallas_call(
        grads_kernel,
        grid=(hot, chunks),
        out_shape=(
            jax.ShapeDtypeStruct((hot, width, hidden), BF16),
            jax.ShapeDtypeStruct((hot, width, hidden), BF16),
            jax.ShapeDtypeStruct((hot, hidden, width), BF16),
        ),
        in_specs=[
            pl.BlockSpec((2, total, width), lambda h, s: (0, 0, 0)),
            pl.BlockSpec((1, 3, total, f), lambda h, s: (h, 0, 0, s)),
        ],
        out_specs=(
            pl.BlockSpec((1, width, f), lambda h, s: (h, 0, s)),
            pl.BlockSpec((1, width, f), lambda h, s: (h, 0, s)),
            pl.BlockSpec((1, f, width), lambda h, s: (h, s, 0)),
        ),
        scratch_shapes=[pltpu.VMEM((width, total), BF16)],
        cost_estimate=pl.CostEstimate(
            flops=6 * hot * total * width * hidden,
            bytes_accessed=6 * hot * width * hidden,
            transcendentals=0,
        ),
        compiler_params=pltpu.CompilerParams(vmem_limit_bytes=48 * 1024 * 1024),
    )(x_all, acts)
    return reduced[:, :width], reduced[:, width:], grad_gate, grad_up, grad_down


def solution(mesh):
    placed = (
        P(("parts", "expert"), "dp"),
        P(("parts", "expert"), "dp"),
        P("parts", "dp", "expert"),
        P("parts", "dp", "expert"),
        P("parts", "expert", "dp"),
        P(),
        P("parts", None),
        P("parts"),
        P("parts"),
    )
    return jax.shard_map(
        functools.partial(local, mesh.shape["expert"]),
        mesh=mesh,
        in_specs=placed,
        out_specs=(
            P(("parts", "expert"), "dp"),
            P(("parts", "expert"), "dp"),
            P("parts", "dp", "expert"),
            P("parts", "dp", "expert"),
            P("parts", "expert", "dp"),
        ),
        check_vma=False,
    )
```

```python
import functools

import jax
import jax.numpy as jnp
from jax import lax
from jax.experimental import pallas as pl
from jax.experimental.pallas import tpu as pltpu
from jax.sharding import PartitionSpec as P

MESH = pl.DeviceIdType.MESH
BF16, F32 = jnp.bfloat16, jnp.float32


def dot(a, b):
    return jnp.dot(a, b, preferred_element_type=F32)


def dot_nt(a, b):
    return lax.dot_general(a, b, (((1,), (1,)), ((), ())), preferred_element_type=F32)


def layer_kernel(
    n_expert, chunks, lead,
    tok_ref, cot_ref, table_ref, ids_ref, index_ref, hot_ref, wg_hbm, wu_hbm, wd_hbm,
    x_out, act_out, *rest,
):
    part_out, rest = rest[:n_expert], rest[n_expert:]
    (wg, wu, wd, xall, own, send1, recv1, send2, recv2, act, acc, part, wt,
     w_sem, x_send, x_recv, s1, r1, s2, r2, s3, r3, out_sem, act_sem, part_sem) = rest
    rows, width = tok_ref.shape
    f = wg.shape[3]
    z = lax.axis_index("expert")
    dp = lax.axis_index("dp")
    mine = lax.rem(dp, 2)
    other = 1 - mine
    near = dp + 1 - 2 * mine
    far = lax.rem(dp + 2, 4)

    def load(k, h, s):
        cols = pl.ds(pl.multiple_of(s * f, f), f)
        if k == 2:
            src, dst = wd_hbm.at[h, cols, :], wd.at[h, s]
        else:
            src, dst = (wg_hbm, wu_hbm)[k].at[h, :, cols], (wg, wu)[k].at[h, s]
        return pltpu.make_async_copy(src, dst, w_sem.at[k, h, s])

    def load_gu(s, carry):
        for h in (other, mine):
            load(0, h, s).start()
            load(1, h, s).start()
        return carry

    def load_down(s, carry):
        for h in (other, mine):
            load(2, h, s).start()
        return carry

    def gather(k, step):
        peer = lax.rem(z + step, n_expert)
        mine_rows = pl.ds(pl.multiple_of(z * rows, rows), rows)
        return pltpu.make_async_remote_copy(
            src_ref=(tok_ref, cot_ref)[k],
            dst_ref=xall.at[k, mine_rows, :],
            send_sem=x_send.at[k, step],
            recv_sem=x_recv.at[k, step],
            device_id={"expert": peer},
            device_id_type=MESH,
        )

    barrier = pltpu.get_barrier_semaphore()

    def greet(step, carry):
        pl.semaphore_signal(
            barrier, inc=1, device_id={"expert": lax.rem(z + step, n_expert)}, device_id_type=MESH
        )
        return carry

    lax.fori_loop(0, lead, load_gu, 0)
    lax.fori_loop(1, n_expert, greet, 0)
    pl.semaphore_signal(barrier, inc=1, device_id={"dp": near}, device_id_type=MESH)
    pl.semaphore_signal(barrier, inc=1, device_id={"dp": far}, device_id_type=MESH)
    pl.semaphore_wait(barrier, n_expert + 1)

    for k in range(2):
        def send_rows(step, carry, k=k):
            gather(k, step).start()
            return carry
        lax.fori_loop(1, n_expert, send_rows, 0)

    def later(s, carry):
        load_down(s, 0)

        @pl.when(s + lead < chunks)
        def _():
            load_gu(s + lead, 0)
        return carry

    lax.fori_loop(0, chunks, later, 0)
    own_rows = pl.ds(pl.multiple_of(z * rows, rows), rows)
    xall[0, own_rows, :] = tok_ref[...]
    xall[1, own_rows, :] = cot_ref[...]
    acc[...] = jnp.zeros_like(acc)

    slots, total = table_ref.shape[1], index_ref.shape[1]
    select = lax.broadcasted_iota(jnp.int32, (slots, total), 0) == index_ref[...]
    even = lax.rem(lax.broadcasted_iota(jnp.int32, (8, slots), 0), 2) == 0
    table = jnp.where(even, table_ref[0:1, :], table_ref[1:2, :]).T
    first_gate, second_gate = (
        jnp.sum(jnp.where(select, table[:, k:k + 1], 0.0), axis=0, keepdims=True) for k in range(2)
    )
    hot = jnp.where(mine == 0, hot_ref[:, 0:1], hot_ref[:, 1:2])
    weight_row = jnp.where(ids_ref[0:1, :] == hot, first_gate, 0.0) + jnp.where(
        ids_ref[1:2, :] == hot, second_gate, 0.0
    )
    wt[...] = jnp.broadcast_to(weight_row, (8, total)).T[:, 0:1]

    def arrive(k):
        def body(step, carry):
            gather(k, step).wait_recv()
            return carry
        lax.fori_loop(1, n_expert, body, 0)
        pltpu.make_async_copy(xall.at[k], x_out.at[k], out_sem.at[k]).start()

    span = (pl.ds(0, 2), pl.ds(2, 1))

    def to_near(g, s):
        return pltpu.make_async_remote_copy(
            src_ref=send1.at[s, span[g]], dst_ref=recv1.at[s, span[g]],
            send_sem=s1.at[g, s], recv_sem=r1.at[g, s],
            device_id={"dp": near}, device_id_type=MESH,
        )

    def to_far(g, s):
        return pltpu.make_async_remote_copy(
            src_ref=send2.at[s, span[g]], dst_ref=recv2.at[s, span[g]],
            send_sem=s2.at[g, s], recv_sem=r2.at[g, s],
            device_id={"dp": far}, device_id_type=MESH,
        )

    def act_to_near(h, s):
        return pltpu.make_async_remote_copy(
            src_ref=act.at[h, s], dst_ref=act.at[h, s],
            send_sem=s3.at[s], recv_sem=r3.at[s],
            device_id={"dp": near}, device_id_type=MESH,
        )

    def act_copy(h, s):
        cols = pl.ds(pl.multiple_of(s * f, f), f)
        return pltpu.make_async_copy(act.at[h, s], act_out.at[h, :, :, cols], act_sem.at[h, s])

    def gate_up(s):
        for k, w in ((0, wg), (1, wu)):
            load(k, other, s).wait()
            send1[s, k] = dot(xall[0], w[other, s]).astype(BF16)
        to_near(0, s).start()
        for k, w in ((0, wg), (1, wu)):
            load(k, mine, s).wait()
            own[s, k] = dot(xall[0], w[mine, s])

    def back(s):
        load(2, other, s).wait()
        send1[s, 2] = dot_nt(xall[1], wd[other, s]).astype(BF16)
        to_near(1, s).start()
        load(2, mine, s).wait()
        own[s, 2] = dot_nt(xall[1], wd[mine, s])

    def pair(g, s):
        to_near(g, s).wait_recv()
        for k in ((0, 1), (2,))[g]:
            both = own[s, k] + recv1[s, k].astype(F32)
            own[s, k] = both
            send2[s, k] = both.astype(BF16)
        to_far(g, s).start()

    arrive(0)

    def first(s, carry):
        @pl.when(s < chunks)
        def _():
            gate_up(s)

        @pl.when((s >= 1) & (s <= chunks))
        def _():
            pair(0, s - 1)

        @pl.when(s == lead)
        def _():
            arrive(1)

        @pl.when((s >= lead) & (s < chunks + lead))
        def _():
            back(s - lead)

        @pl.when(s >= lead + 1)
        def _():
            pair(1, s - lead - 1)
        return carry

    lax.fori_loop(0, chunks + lead + 1, first, 0)

    def project(h, s):
        acc[0] += dot(act[h, s, 0], wd[h, s])
        acc[1] += dot_nt(act[h, s, 1], wg[h, s]) + dot_nt(act[h, s, 2], wu[h, s])

    def second(s, carry):
        @pl.when(s < chunks)
        def _():
            to_far(0, s).wait_recv()
            to_far(1, s).wait_recv()
            weight = wt[...]
            gate = own[s, 0] + recv2[s, 0].astype(F32)
            up = own[s, 1] + recv2[s, 1].astype(F32)
            scaled = weight * (own[s, 2] + recv2[s, 2].astype(F32))
            sigma = jax.nn.sigmoid(gate)
            silu = gate * sigma
            act[mine, s, 0] = (weight * silu * up).astype(BF16)
            act[mine, s, 1] = (scaled * up * (sigma * (1.0 + gate * (1.0 - sigma)))).astype(BF16)
            act[mine, s, 2] = (scaled * silu).astype(BF16)
            act_to_near(mine, s).start()
            act_copy(mine, s).start()
            project(mine, s)

        @pl.when(s >= 1)
        def _():
            act_to_near(other, s - 1).wait_recv()
            act_copy(other, s - 1).start()
            project(other, s - 1)
        return carry

    lax.fori_loop(0, chunks + 1, second, 0)

    part[:, :width] = acc[0].astype(BF16)
    part[:, width:] = acc[1].astype(BF16)
    copies = []
    for step in range(n_expert):
        to_rows = pl.ds(pl.multiple_of(lax.rem(z + step, n_expert) * rows, rows), rows)
        copies.append(pltpu.make_async_copy(part.at[to_rows, :], part_out[step], part_sem.at[step]))
        copies[-1].start()

    def drain(s, carry):
        for g in range(2):
            to_near(g, s).wait_send()
            to_far(g, s).wait_send()
        act_to_near(mine, s).wait_send()
        for h in range(2):
            act_copy(h, s).wait()
        return carry

    lax.fori_loop(0, chunks, drain, 0)

    def drain_rows(step, carry):
        for k in range(2):
            gather(k, step).wait_send()
        return carry

    lax.fori_loop(1, n_expert, drain_rows, 0)
    for k in range(2):
        pltpu.make_async_copy(xall.at[k], x_out.at[k], out_sem.at[k]).wait()
    for copy in copies:
        copy.wait()


def grads_kernel(x_ref, act_ref, gg_ref, gu_ref, gd_ref, tok_t):
    @pl.when((pl.program_id(0) == 0) & (pl.program_id(1) == 0))
    def _():
        tok_t[...] = x_ref[0].T

    gg_ref[0] = dot(tok_t[...], act_ref[0, 1]).astype(BF16)
    gu_ref[0] = dot(tok_t[...], act_ref[0, 2]).astype(BF16)
    gd_ref[0] = dot(act_ref[0, 0].T, x_ref[1]).astype(BF16)


def local(n_expert, tokens, cotangent, w_gate, w_up, w_down, gate_table, expert_ids, gate_index, hot_ids):
    rows, width = tokens.shape
    hot, _, hidden = w_gate.shape
    total = rows * n_expert
    f = min(256, hidden)
    chunks = hidden // f
    lead = chunks // 2
    vmem, anywhere = pl.BlockSpec(memory_space=pltpu.VMEM), pl.BlockSpec(memory_space=pl.ANY)
    dma = pltpu.SemaphoreType.DMA
    x_all, acts, *blocks = pl.pallas_call(
        functools.partial(layer_kernel, n_expert, chunks, lead),
        out_shape=(
            jax.ShapeDtypeStruct((2, total, width), BF16),
            jax.ShapeDtypeStruct((hot, 3, total, hidden), BF16),
        ) + (jax.ShapeDtypeStruct((rows, 2 * width), BF16),) * n_expert,
        in_specs=[vmem] * 6 + [anywhere] * 3,
        out_specs=(anywhere,) * (2 + n_expert),
        scratch_shapes=[
            pltpu.VMEM((hot, chunks, width, f), BF16),
            pltpu.VMEM((hot, chunks, width, f), BF16),
            pltpu.VMEM((hot, chunks, f, width), BF16),
            pltpu.VMEM((2, total, width), BF16),
            pltpu.VMEM((chunks, 3, total, f), F32),
            pltpu.VMEM((chunks, 3, total, f), BF16),
            pltpu.VMEM((chunks, 3, total, f), BF16),
            pltpu.VMEM((chunks, 3, total, f), BF16),
            pltpu.VMEM((chunks, 3, total, f), BF16),
            pltpu.VMEM((hot, chunks, 3, total, f), BF16),
            pltpu.VMEM((2, total, width), F32),
            pltpu.VMEM((total, 2 * width), BF16),
            pltpu.VMEM((total, 1), F32),
            dma((3, hot, chunks)),
            dma((2, n_expert)),
            dma((2, n_expert)),
            dma((2, chunks)),
            dma((2, chunks)),
            dma((2, chunks)),
            dma((2, chunks)),
            dma((chunks,)),
            dma((chunks,)),
            dma((2,)),
            dma((hot, chunks)),
            dma((n_expert,)),
        ],
        compiler_params=pltpu.CompilerParams(
            collective_id=0, has_side_effects=True, vmem_limit_bytes=60 * 1024 * 1024
        ),
    )(
        tokens, cotangent, gate_table.T, expert_ids.T,
        gate_index.reshape(1, total), hot_ids.reshape(1, hot), w_gate, w_up, w_down,
    )
    arrived = [
        lax.ppermute(block, "expert", [(i, (i + step) % n_expert) for i in range(n_expert)])
        for step, block in enumerate(blocks) if step > 0
    ]
    wide = min(512, hidden)
    grad_gate, grad_up, grad_down = pl.pallas_call(
        grads_kernel,
        grid=(hot, hidden // wide),
        out_shape=(
            jax.ShapeDtypeStruct((hot, width, hidden), BF16),
            jax.ShapeDtypeStruct((hot, width, hidden), BF16),
            jax.ShapeDtypeStruct((hot, hidden, width), BF16),
        ),
        in_specs=[
            pl.BlockSpec((2, total, width), lambda h, s: (0, 0, 0)),
            pl.BlockSpec((1, 3, total, wide), lambda h, s: (h, 0, 0, s)),
        ],
        out_specs=(
            pl.BlockSpec((1, width, wide), lambda h, s: (h, 0, s)),
            pl.BlockSpec((1, width, wide), lambda h, s: (h, 0, s)),
            pl.BlockSpec((1, wide, width), lambda h, s: (h, s, 0)),
        ),
        scratch_shapes=[pltpu.VMEM((width, total), BF16)],
        cost_estimate=pl.CostEstimate(
            flops=6 * hot * total * width * hidden,
            bytes_accessed=6 * hot * width * hidden,
            transcendentals=0,
        ),
        compiler_params=pltpu.CompilerParams(vmem_limit_bytes=60 * 1024 * 1024),
    )(x_all, acts)
    mixed, grad_tokens = (
        functools.reduce(
            jnp.add, [block[:, half].astype(F32) for block in [blocks[0]] + arrived]
        ).astype(BF16)
        for half in (slice(0, width), slice(width, None))
    )
    return mixed, grad_tokens, grad_gate, grad_up, grad_down


def solution(mesh):
    placed = (
        P(("parts", "expert"), "dp"),
        P(("parts", "expert"), "dp"),
        P("parts", "dp", "expert"),
        P("parts", "dp", "expert"),
        P("parts", "expert", "dp"),
        P(),
        P("parts", None),
        P("parts"),
        P("parts"),
    )
    return jax.shard_map(
        functools.partial(local, mesh.shape["expert"]),
        mesh=mesh,
        in_specs=placed,
        out_specs=(
            P(("parts", "expert"), "dp"),
            P(("parts", "expert"), "dp"),
            P("parts", "dp", "expert"),
            P("parts", "dp", "expert"),
            P("parts", "expert", "dp"),
        ),
        check_vma=False,
    )
```
